32 devices in a mesh: particle: 8 (over z, x), band: 4 (over y, core).
Axes of the slice: x: 2, y: 2, z: 4, core: 2. Of those that a mesh axis runs over, the one named last changes fastest.
Arguments:
- states: float32 [32, 2, 64, 1024], P('particle', None, 'band'), may hold values from -4 to 4
- counts: int32 [32], replicated, may hold values from 0 to 2, as said below
Outputs:
- forecast: float32 [32, 2, 64, 1024], P('particle', None, 'band')
The draws below stay inside these ranges and needn't reach their ends.
Inputs may be any that keep to these rules, and one draw needn't show every extreme that they name: Counts sum to 32; particle 0 and particle 32 - 1 have count 1, and for every m the particles 2m + 1 and 2m + 2 have counts summing to 2, so each slot's ancestor is the slot itself or a particle next to it; where 2m + 2 is a multiple of 4, the pair's counts are (2, 0).
All inputs are finite; a program needn't handle non-finite values.
Results may differ from the reference program's by a relative error of at most 0.00002.
Values sent between devices are 32-bit elements; how exact they have to be, the bound alone decides.
A program may use at most 64 MiB of HBM per device.

```python
import jax
import jax.numpy as jnp
from jax import lax

P_DEV = 4
NX = 1024
GRID_HIERARCHY = 3
COARSE_SWEEPS = 6
NP = 32
NY = 64


def draw_counts(key, part):
    pair_count = NP // 2 - 1
    first_particle = 2 * jnp.arange(pair_count, dtype=jnp.int32) + 2
    straddle = first_particle % P_DEV == 0
    unbound_layout = jax.random.randint(jax.random.fold_in(key, 11), (pair_count,), 0, 3)
    pattern = jnp.where(straddle, 1, unbound_layout)
    leading = jnp.where(pattern == 0, 1, jnp.where(pattern == 1, 2, 0)).astype(jnp.int32)
    trailing = (2 - leading).astype(jnp.int32)
    middle = jnp.stack([leading, trailing], axis=1).reshape(-1)
    single = jnp.ones((1,), jnp.int32)
    return jnp.concatenate([single, middle, single])


def draw_states(key, part):
    domain_span = (NP, 2, NY, NX)
    noise = jax.random.normal(jax.random.fold_in(key, 22), domain_span, jnp.float32)
    return jnp.clip(noise, -4.0, 4.0)


def setup_inputs(seed: int = 0) -> dict:
    arg_keys = jax.random.split(jax.random.key(seed), 3)
    states = draw_states(jax.random.fold_in(arg_keys[2], 71), 0)
    counts = draw_counts(jax.random.fold_in(arg_keys[2], 71), 0)
    return {"states": states, "counts": counts}


smoothing_weight = 0.8
deform_term = 0.1
beta_slope = 0.5
bottom_friction_coefficient = 0.2
time_step = 0.5
meridional_weight = 1.8
zonal_weight = 0.2


def zero_rows(field):
    border = jnp.zeros_like(field[..., :1, :])
    return jnp.concatenate([border, field, border], axis=-2)


def neighbours(field, widened_field):
    across = widened_field[..., 2:, :] + widened_field[..., :-2, :]
    along = jnp.roll(field, -1, axis=-1) + jnp.roll(field, 1, axis=-1)
    return meridional_weight * across + zonal_weight * along


def smooth(field, forcing_term, diagonal_term):
    applied = diagonal_term * field - neighbours(field, zero_rows(field))
    return field + smoothing_weight * (forcing_term - applied) / diagonal_term


def restrict(field):
    leading = field.shape[:-2]
    height, breadth = field.shape[-2], field.shape[-1]
    blocks = field.reshape(leading + (height // 2, 2, breadth // 2, 2))
    return jnp.sum(blocks, axis=(-3, -1))


def prolong(field):
    return jnp.repeat(jnp.repeat(field, 2, axis=-2), 2, axis=-1)


def diagonal_at(level):
    return 4.0 + jnp.array([0.0, deform_term], jnp.float32).reshape(2, 1, 1) * (4.0 ** level)


def cycle(forcing_term, level):
    diagonal_term = diagonal_at(level)
    field = smoothing_weight * forcing_term / diagonal_term
    if level == GRID_HIERARCHY - 1:
        for repeat in range(COARSE_SWEEPS - 1):
            field = smooth(field, forcing_term, diagonal_term)
        return field
    field = smooth(field, forcing_term, diagonal_term)
    remainder = forcing_term - (diagonal_term * field - neighbours(field, zero_rows(field)))
    field = field + prolong(cycle(restrict(remainder), level + 1))
    field = smooth(field, forcing_term, diagonal_term)
    field = smooth(field, forcing_term, diagonal_term)
    return field


def advance_step(potential_curl_grid, stream, padded_stream, padded_vorticity):
    stream_x = 0.5 * (jnp.roll(stream, -1, axis=-1) - jnp.roll(stream, 1, axis=-1))
    meridional_streamfunction_gradient = 0.5 * (padded_stream[..., 2:, :] - padded_stream[..., :-2, :])
    vort_x = 0.5 * (jnp.roll(potential_curl_grid, -1, axis=-1) - jnp.roll(potential_curl_grid, 1, axis=-1))
    vort_y = 0.5 * (padded_vorticity[..., 2:, :] - padded_vorticity[..., :-2, :])
    laplace = neighbours(stream, padded_stream) - 4.0 * stream
    drag = jnp.array([0.0, bottom_friction_coefficient], jnp.float32).reshape(2, 1, 1)
    jacobian = stream_x * vort_y - meridional_streamfunction_gradient * vort_x
    return potential_curl_grid - time_step * (jacobian + beta_slope * stream_x + drag * laplace)


def lone_prediction_update(potential_curl_grid):
    upper = potential_curl_grid[..., 0, :, :]
    lower = potential_curl_grid[..., 1, :, :]
    forcing_term = -jnp.stack([0.5 * (upper + lower), 0.5 * (upper - lower)], axis=-3)
    modes = cycle(forcing_term, 0)
    stream = jnp.stack([modes[..., 0, :, :] + modes[..., 1, :, :], modes[..., 0, :, :] - modes[..., 1, :, :]], axis=-3)
    return advance_step(potential_curl_grid, stream, zero_rows(stream), zero_rows(potential_curl_grid))


def reference(states, counts):
    totals = jnp.cumsum(counts, dtype=jnp.int32)
    slots = jnp.arange(NP, dtype=jnp.int32)
    ancestor = jnp.sum((totals[None, :] <= slots[:, None]).astype(jnp.int32), axis=1, dtype=jnp.int32)
    redrawn_ensemble = jnp.take(states, ancestor, axis=0)
    return lax.map(lone_prediction_update, redrawn_ensemble)
```

```python
import functools

import jax
import jax.numpy as jnp
from jax import lax
from jax.experimental import pallas as pl
from jax.experimental.pallas import tpu as pltpu
from jax.sharding import PartitionSpec as P

MESH = pl.DeviceIdType.MESH
DEFORM = 0.1
RELAX = 0.8
BETA = 0.5
DRAG = 0.2
STEP = 0.5
WY = 1.8
WX = 0.2
H0 = 6
H1 = 5
HC = 8


def lane_roll(a, steps):
    return pltpu.roll(a, steps % a.shape[-1], axis=a.ndim - 1)


def sides(row):
    n = len(row)
    left = [row[r - 1] if r else lane_roll(row[n - 1], 1) for r in range(n)]
    right = [row[r + 1] if r < n - 1 else lane_roll(row[0], -1) for r in range(n)]
    return left, right


def nb(above, row, below):
    left, right = sides(row)
    return [
        WY * (above[r] + below[r]) + WX * (left[r] + right[r]) for r in range(len(row))
    ]


def kernel(bands, groups, slots, rows, counts, x_hbm, out_hbm,
           xv, ov, fwd, inv, tr, q, s0, f0, g0, h0, s1, f1, g1, h1, s2, c2a, c2b,
           in_sem, out_sem, send_sem, recv_sem):
    band = lax.axis_index("band")
    group = lax.axis_index("particle")
    rows1, rows2 = rows // 2, rows // 4
    has = [band >= 1, band >= 2, band < bands - 1, band < bands - 2]
    offsets = [-1, -2, 1, 2]
    below, above = group >= 1, group < groups - 1

    barrier = pltpu.get_barrier_semaphore()
    expected = jnp.int32(0)
    for ok, off in zip(has, offsets):
        expected += jnp.where(ok, 1, 0)

        @pl.when(ok)
        def _():
            pl.semaphore_signal(barrier, inc=1, device_id=(group, band + off), device_id_type=MESH)
    for ok, off in ((below, -1), (above, 1)):
        expected += jnp.where(ok, 1, 0)

        @pl.when(ok)
        def _():
            pl.semaphore_signal(barrier, inc=1, device_id=(group + off, band), device_id_type=MESH)

    loads = [pltpu.make_async_copy(x_hbm.at[j], xv.at[j], in_sem.at[j]) for j in range(slots)]
    for c in loads:
        c.start()

    size = fwd.shape[0]
    quarter = size // 4
    i0 = lax.broadcasted_iota(jnp.int32, (size, size), 0)
    i1 = lax.broadcasted_iota(jnp.int32, (size, size), 1)
    fwd[...] = jnp.where(i0 == 4 * (i1 % quarter) + i1 // quarter, 1.0, 0.0).astype(jnp.bfloat16)
    inv[...] = jnp.where(i1 == 4 * (i0 % quarter) + i0 // quarter, 1.0, 0.0).astype(jnp.bfloat16)

    first = group * slots
    total = jnp.int32(0)
    ancestor = [jnp.int32(0)] * slots
    for i in range(counts.shape[0]):
        total = total + counts[i]
        for j in range(slots):
            ancestor[j] = ancestor[j] + jnp.where(total <= first + j, 1, 0)
    local = [jnp.clip(a - first, 0, slots - 1) for a in ancestor]

    zero = lambda ref, lo, n: ref.__setitem__(pl.ds(lo, n), jnp.zeros((n,) + ref.shape[1:], jnp.float32))

    @pl.when(band == 0)
    def _():
        zero(q, 0, H0)
        zero(s1, 0, 3)
        zero(s2, HC - rows2, rows2)

    @pl.when(band <= 1)
    def _():
        zero(s2, HC - 2 * rows2, rows2)

    @pl.when(band == bands - 1)
    def _():
        zero(q, H0 + rows, H0)
        zero(s1, H1 + rows1 + 2, 3)
        zero(s2, HC + rows2, rows2)

    @pl.when(band >= bands - 2)
    def _():
        zero(s2, HC + 2 * rows2, rows2)

    for c in loads:
        c.wait()

    blocks = xv.shape[-1] // size
    for kb in range(blocks):
        cols = pl.ds(kb * size, size)
        a = jnp.concatenate([xv[local[s], l, :, cols] for l in range(2) for s in range(slots)], axis=0)
        hi = a.astype(jnp.bfloat16)
        lo = (a - hi.astype(jnp.float32)).astype(jnp.bfloat16)
        o = jnp.dot(hi, fwd[...], preferred_element_type=jnp.float32)
        o = o + jnp.dot(lo, fwd[...], preferred_element_type=jnp.float32)
        for r in range(4):
            tr[r, kb] = o[:, r * quarter:(r + 1) * quarter]

    lanes = blocks * quarter
    for y in range(rows):
        for r in range(4):
            for kb in range(blocks):
                q[H0 + y, r, :, kb * quarter:(kb + 1) * quarter] = tr[r, kb, pl.ds(y, 8, stride=rows), :]

    pl.semaphore_wait(barrier, expected)

    def remote(src, dst, sem, dev):
        return pltpu.make_async_remote_copy(
            src_ref=src, dst_ref=dst, send_sem=send_sem.at[sem], recv_sem=recv_sem.at[sem],
            device_id=dev, device_id_type=MESH)

    halo_down = remote(q.at[pl.ds(H0, H0)], q.at[pl.ds(H0 + rows, H0)], 0, (group, band - 1))
    halo_up = remote(q.at[pl.ds(rows, H0)], q.at[pl.ds(0, H0)], 1, (group, band + 1))
    pl.when(has[0])(halo_down.start)
    pl.when(has[2])(halo_up.start)

    sub = lax.broadcasted_iota(jnp.int32, (8, lanes), 0) >= slots
    sgn = jnp.where(sub, -1.0, 1.0).astype(jnp.float32)

    def diag(level):
        d = jnp.where(sub, 4.0 + DEFORM * 4.0 ** level, 4.0).astype(jnp.float32)
        return d, RELAX / d

    def swap(v):
        return pltpu.roll(v, slots, axis=0)

    def get(ref, i):
        return [ref[i, r] for r in range(ref.shape[1])]

    def put(ref, i, vals, mask):
        for r, v in enumerate(vals):
            ref[i, r] = v if mask is None else v * mask

    top = jnp.where(band == 0, 0.0, 1.0).astype(jnp.float32)
    bot = jnp.where(band == bands - 1, 0.0, 1.0).astype(jnp.float32)

    def over(lo, n, hi, body, unroll=2):
        for a, b, mask, u in ((lo, 0, top, 1), (0, n, None, unroll), (n, hi, bot, 1)):
            if b > a:
                def step(i, carry, mask=mask):
                    body(i, mask)
                    return carry
                lax.fori_loop(a, b, step, 0, unroll=u)

    pl.when(has[2])(halo_down.wait_recv)
    pl.when(has[0])(halo_up.wait_recv)

    d0, w0 = diag(0)

    def source(i, mask):
        row = get(q, H0 + i)
        put(s0, H0 + i, [-0.5 * (swap(v) + sgn * v) for v in row], None)
    over(-H0, rows, rows + H0, source)

    def pre(s_ref, f_ref, off, w):
        wa, wb = 1.2 * w, w * w

        def body(i, mask):
            row = get(s_ref, off + i)
            n = nb(get(s_ref, off + i - 1), row, get(s_ref, off + i + 1))
            put(f_ref, off + i, [wa * s + wb * v for s, v in zip(row, n)], mask)
        return body

    over(-5, rows, rows + 5, pre(s0, f0, H0, w0))

    def residual(s_ref, f_ref, off, d):
        def rest(i):
            row = get(f_ref, off + i)
            n = nb(get(f_ref, off + i - 1), row, get(f_ref, off + i + 1))
            return [s - d * f + v for s, f, v in zip(get(s_ref, off + i), row, n)]

        def coarse(i):
            a, b = rest(2 * i), rest(2 * i + 1)
            c = [x + y for x, y in zip(a, b)]
            return [c[2 * r] + c[2 * r + 1] for r in range(len(c) // 2)]
        return coarse

    coarse0 = residual(s0, f0, H0, d0)
    over(-2, rows1, rows1 + 2, lambda i, mask: put(s1, H1 + i, coarse0(i), mask), 1)

    one_down = remote(s1.at[pl.ds(H1 + 2, 3)], s1.at[pl.ds(H1 + rows1 + 2, 3)], 2, (group, band - 1))
    one_up = remote(s1.at[pl.ds(H1 + rows1 - 5, 3)], s1.at[pl.ds(0, 3)], 3, (group, band + 1))
    pl.when(has[0])(one_down.start)
    pl.when(has[2])(one_up.start)

    d1, w1 = diag(1)
    pre1 = pre(s1, f1, H1, w1)
    over(-1, rows1, rows1 + 1, pre1)
    coarse1 = residual(s1, f1, H1, d1)
    over(0, rows2, rows2, lambda i, mask: put(s2, HC + i, coarse1(i), mask), 1)

    own2 = s2.at[pl.ds(HC, rows2)]
    gather = []
    for n, (ok, off) in enumerate(zip(has, offsets)):
        c = remote(own2, s2.at[pl.ds(HC - off * rows2, rows2)], 4 + n, (group, band + off))
        pl.when(ok)(c.start)
        gather.append(c)

    pl.when(has[2])(one_down.wait_recv)
    pl.when(has[0])(one_up.wait_recv)

    def outer(a, b, mask):
        def step(i, carry):
            pre1(i, mask)
            return carry
        lax.fori_loop(a, b, step, 0)
    outer(-4, -1, top)
    outer(rows1 + 1, rows1 + 4, bot)

    for n, src in enumerate((2, 3, 0, 1)):
        pl.when(has[src])(gather[n].wait_recv)

    d2, w2 = diag(2)
    far_top = jnp.where(band <= 1, 0.0, 1.0).astype(jnp.float32)
    far_bot = jnp.where(band >= bands - 2, 0.0, 1.0).astype(jnp.float32)

    def mask2(i):
        if i < 0:
            return top if i >= -rows2 else far_top
        if i >= rows2:
            return bot if i < 2 * rows2 else far_bot
        return None

    body = pre(s2, c2a, HC, w2)
    for i in range(-6, rows2 + 6):
        body(i, mask2(i))

    def sweep(s_ref, f_ref, o_ref, off, w):
        def body(i, mask):
            row = get(f_ref, off + i)
            n = nb(get(f_ref, off + i - 1), row, get(f_ref, off + i + 1))
            put(o_ref, off + i, [0.2 * f + w * (s + v) for s, f, v in zip(get(s_ref, off + i), row, n)], mask)
        return body

    a, b = c2a, c2b
    for reach in (5, 4, 3, 2):
        body = sweep(s2, a, b, HC, w2)
        for i in range(-reach, rows2 + reach):
            body(i, mask2(i))
        a, b = b, a
    e2 = a

    def add1(i, mask):
        for t in range(2):
            e = e2[HC + i, 0]
            put(g1, H1 + 2 * i + t, [v + e for v in get(f1, H1 + 2 * i + t)], None)
    over(-2, rows2, rows2 + 2, add1)
    over(-3, rows1, rows1 + 3, sweep(s1, g1, h1, H1, w1))
    over(-2, rows1, rows1 + 2, sweep(s1, h1, g1, H1, w1))

    def add0(i, mask):
        e = get(g1, H1 + i)
        for t in range(2):
            v = get(f0, H0 + 2 * i + t)
            put(g0, H0 + 2 * i + t, [v[r] + e[r // 2] for r in range(4)], None)
    over(-2, rows1, rows1 + 2, add0)
    over(-2, rows, rows + 2, sweep(s0, g0, h0, H0, w0))
    last = sweep(s0, h0, g0, H0, w0)
    over(-1, rows, rows + 1, last)

    def to_stream(i, mask):
        put(h0, H0 + i, [swap(v) + sgn * v for v in get(g0, H0 + i)], None)
    over(-1, rows, rows + 1, to_stream)

    drag = jnp.where(sub, DRAG, 0.0).astype(jnp.float32)

    def advance(i, mask):
        st, su, sd = get(h0, H0 + i), get(h0, H0 + i - 1), get(h0, H0 + i + 1)
        qq, qu, qd = get(q, H0 + i), get(q, H0 + i - 1), get(q, H0 + i + 1)
        sl, sr = sides(st)
        ql, qr = sides(qq)
        for r in range(4):
            sx = 0.5 * (sr[r] - sl[r])
            sy = 0.5 * (sd[r] - su[r])
            qx = 0.5 * (qr[r] - ql[r])
            qy = 0.5 * (qd[r] - qu[r])
            lap = WY * (su[r] + sd[r]) + WX * (sl[r] + sr[r]) - 4.0 * st[r]
            v = qq[r] - STEP * (sx * qy - sy * qx + BETA * sx + drag * lap)
            for kb in range(blocks):
                tr[r, kb, pl.ds(i, 8, stride=rows), :] = v[:, kb * quarter:(kb + 1) * quarter]
    over(0, rows, rows, advance, 1)

    for kb in range(blocks):
        a = jnp.concatenate([tr[r, kb] for r in range(4)], axis=1)
        hi = a.astype(jnp.bfloat16)
        lo = (a - hi.astype(jnp.float32)).astype(jnp.bfloat16)
        o = jnp.dot(hi, inv[...], preferred_element_type=jnp.float32)
        o = o + jnp.dot(lo, inv[...], preferred_element_type=jnp.float32)
        for l in range(2):
            for s in range(slots):
                n = (l * slots + s) * rows
                ov[s, l, :, kb * size:(kb + 1) * size] = o[n:n + rows]

    share = remote(ov.at[slots - 1], out_hbm.at[0], 8, (group + 1, band))
    pl.when(above)(share.start)
    stores = [pltpu.make_async_copy(ov.at[j], out_hbm.at[j], out_sem.at[j]) for j in range(slots)]
    for c in stores[1:]:
        c.start()
    pl.when(group == 0)(stores[0].start)
    for c in stores[1:]:
        c.wait()
    pl.when(group == 0)(stores[0].wait)
    for ok, c in ((has[0], halo_down), (has[2], halo_up), (has[0], one_down), (has[2], one_up),
                  (above, share), *zip(has, gather)):
        pl.when(ok)(c.wait_send)
    pl.when(below)(share.wait_recv)


def per_device(states, counts):
    slots, layers, rows, nx = states.shape
    bands, groups = lax.axis_size("band"), lax.axis_size("particle")
    rows1, rows2, lanes = rows // 2, rows // 4, nx // 4
    f32 = jnp.float32
    level0 = pltpu.VMEM((rows + 2 * H0, 4, 8, lanes), f32)
    level1 = pltpu.VMEM((rows1 + 2 * H1, 2, 8, lanes), f32)
    level2 = pltpu.VMEM((rows2 + 2 * HC, 1, 8, lanes), f32)
    return pl.pallas_call(
        functools.partial(kernel, bands, groups, slots, rows),
        out_shape=jax.ShapeDtypeStruct(states.shape, states.dtype),
        in_specs=[pl.BlockSpec(memory_space=pltpu.SMEM), pl.BlockSpec(memory_space=pl.ANY)],
        out_specs=pl.BlockSpec(memory_space=pl.ANY),
        scratch_shapes=[
            pltpu.VMEM(states.shape, f32),
            pltpu.VMEM(states.shape, f32),
            pltpu.VMEM((512, 512), jnp.bfloat16),
            pltpu.VMEM((512, 512), jnp.bfloat16),
            pltpu.VMEM((4, nx // 512, 8 * rows, 128), f32),
            level0, level0, level0, level0, level0,
            level1, level1, level1, level1,
            level2, level2, level2,
            pltpu.SemaphoreType.DMA((slots,)),
            pltpu.SemaphoreType.DMA((slots,)),
            pltpu.SemaphoreType.DMA((9,)),
            pltpu.SemaphoreType.DMA((9,)),
        ],
        compiler_params=pltpu.CompilerParams(
            collective_id=0, has_side_effects=True, vmem_limit_bytes=40 * 1024 * 1024
        ),
    )(counts, states)


def solution(mesh):
    in_specs = (P("particle", None, "band", None), P())
    out_specs = P("particle", None, "band", None)
    return jax.shard_map(
        per_device, mesh=mesh, in_specs=in_specs, out_specs=out_specs, check_vma=False
    )
```

```python
import functools

import jax
import jax.numpy as jnp
from jax import lax
from jax.experimental import pallas as pl
from jax.experimental.pallas import tpu as pltpu
from jax.sharding import PartitionSpec as P

MESH = pl.DeviceIdType.MESH
DEFORM = 0.1
RELAX = 0.8
BETA = 0.5
DRAG = 0.2
STEP = 0.5
WY = 1.8
WX = 0.2
H0 = 6
H1 = 5
HC = 8


def lane_roll(a, steps):
    return pltpu.roll(a, steps % a.shape[-1], axis=a.ndim - 1)


def sides(row):
    n = len(row)
    left = [row[r - 1] if r else lane_roll(row[n - 1], 1) for r in range(n)]
    right = [row[r + 1] if r < n - 1 else lane_roll(row[0], -1) for r in range(n)]
    return left, right


def nb(above, row, below):
    left, right = sides(row)
    return [
        WY * (above[r] + below[r]) + WX * (left[r] + right[r]) for r in range(len(row))
    ]


def kernel(bands, groups, slots, rows, counts, x_hbm, out_hbm,
           xv, ov, fwd, inv, tr, q, s0, f0, g0, h0, st0, s1, f1, g1, h1, s2, c2a, c2b,
           in_sem, out_sem, send_sem, recv_sem):
    band = lax.axis_index("band")
    group = lax.axis_index("particle")
    rows1, rows2 = rows // 2, rows // 4
    has = [band >= 1, band >= 2, band < bands - 1, band < bands - 2]
    offsets = [-1, -2, 1, 2]
    below, above = group >= 1, group < groups - 1

    barrier = pltpu.get_barrier_semaphore()
    expected = jnp.int32(0)
    for ok, off in zip(has, offsets):
        expected += jnp.where(ok, 1, 0)

        @pl.when(ok)
        def _():
            pl.semaphore_signal(barrier, inc=1, device_id=(group, band + off), device_id_type=MESH)
    for ok, off in ((below, -1), (above, 1)):
        expected += jnp.where(ok, 1, 0)

        @pl.when(ok)
        def _():
            pl.semaphore_signal(barrier, inc=1, device_id=(group + off, band), device_id_type=MESH)

    loads = [pltpu.make_async_copy(x_hbm.at[j], xv.at[j], in_sem.at[j]) for j in range(slots)]
    for c in loads:
        c.start()

    size = fwd.shape[0]
    quarter = size // 4
    i0 = lax.broadcasted_iota(jnp.int32, (size, size), 0)
    i1 = lax.broadcasted_iota(jnp.int32, (size, size), 1)
    fwd[...] = jnp.where(i0 == 4 * (i1 % quarter) + i1 // quarter, 1.0, 0.0).astype(jnp.bfloat16)
    inv[...] = jnp.where(i1 == 4 * (i0 % quarter) + i0 // quarter, 1.0, 0.0).astype(jnp.bfloat16)

    first = group * slots
    total = jnp.int32(0)
    ancestor = [jnp.int32(0)] * slots
    for i in range(counts.shape[0]):
        total = total + counts[i]
        for j in range(slots):
            ancestor[j] = ancestor[j] + jnp.where(total <= first + j, 1, 0)
    local = [jnp.clip(a - first, 0, slots - 1) for a in ancestor]

    zero = lambda ref, lo, n: ref.__setitem__(pl.ds(lo, n), jnp.zeros((n,) + ref.shape[1:], jnp.float32))

    @pl.when(band == 0)
    def _():
        zero(q, 0, H0)
        zero(s1, 0, 3)
        zero(s2, HC - rows2, rows2)

    @pl.when(band <= 1)
    def _():
        zero(s2, HC - 2 * rows2, rows2)

    @pl.when(band == bands - 1)
    def _():
        zero(q, H0 + rows, H0)
        zero(s1, H1 + rows1 + 2, 3)
        zero(s2, HC + rows2, rows2)

    @pl.when(band >= bands - 2)
    def _():
        zero(s2, HC + 2 * rows2, rows2)

    for c in loads:
        c.wait()

    blocks = xv.shape[-1] // size
    for kb in range(blocks):
        cols = pl.ds(kb * size, size)
        a = jnp.concatenate([xv[local[s], l, :, cols] for l in range(2) for s in range(slots)], axis=0)
        hi = a.astype(jnp.bfloat16)
        lo = (a - hi.astype(jnp.float32)).astype(jnp.bfloat16)
        o = jnp.dot(hi, fwd[...], preferred_element_type=jnp.float32)
        o = o + jnp.dot(lo, fwd[...], preferred_element_type=jnp.float32)
        for r in range(4):
            tr[r, kb] = o[:, r * quarter:(r + 1) * quarter]

    lanes = blocks * quarter
    for y in range(rows):
        for r in range(4):
            for kb in range(blocks):
                q[H0 + y, r, :, kb * quarter:(kb + 1) * quarter] = tr[r, kb, pl.ds(y, 8, stride=rows), :]

    pl.semaphore_wait(barrier, expected)

    def remote(src, dst, sem, dev):
        return pltpu.make_async_remote_copy(
            src_ref=src, dst_ref=dst, send_sem=send_sem.at[sem], recv_sem=recv_sem.at[sem],
            device_id=dev, device_id_type=MESH)

    halo_down = remote(q.at[pl.ds(H0, H0)], q.at[pl.ds(H0 + rows, H0)], 0, (group, band - 1))
    halo_up = remote(q.at[pl.ds(rows, H0)], q.at[pl.ds(0, H0)], 1, (group, band + 1))
    pl.when(has[0])(halo_down.start)
    pl.when(has[2])(halo_up.start)

    sub = lax.broadcasted_iota(jnp.int32, (8, lanes), 0) >= slots
    sgn = jnp.where(sub, -1.0, 1.0).astype(jnp.float32)

    def diag(level):
        d = jnp.where(sub, 4.0 + DEFORM * 4.0 ** level, 4.0).astype(jnp.float32)
        return d, RELAX / d

    def swap(v):
        return pltpu.roll(v, slots, axis=0)

    def get(ref, i):
        return [ref[i, r] for r in range(ref.shape[1])]

    def put(ref, i, vals, mask):
        for r, v in enumerate(vals):
            ref[i, r] = v if mask is None else v * mask

    top = jnp.where(band == 0, 0.0, 1.0).astype(jnp.float32)
    bot = jnp.where(band == bands - 1, 0.0, 1.0).astype(jnp.float32)

    def over(lo, n, hi, body, unroll=4):
        parts = ((lo, min(hi, 0), top, True), (max(lo, 0), min(hi, n), None, unroll),
                 (max(lo, n), hi, bot, True))
        for a, b, mask, u in parts:
            if b > a:
                def step(i, carry, mask=mask):
                    body(i, mask)
                    return carry
                if u is not True:
                    u = max(k for k in range(1, u + 1) if (b - a) % k == 0)
                lax.fori_loop(a, b, step, 0, unroll=u)

    d0, w0 = diag(0)

    def source(i, mask):
        row = get(q, H0 + i)
        put(s0, H0 + i, [-0.5 * (swap(v) + sgn * v) for v in row], None)
    over(0, rows, rows, source)

    def pre(s_ref, f_ref, off, w):
        wa, wb = 1.2 * w, w * w

        def body(i, mask):
            row = get(s_ref, off + i)
            n = nb(get(s_ref, off + i - 1), row, get(s_ref, off + i + 1))
            put(f_ref, off + i, [wa * s + wb * v for s, v in zip(row, n)], mask)
        return body

    pre0 = pre(s0, f0, H0, w0)
    over(1, rows, rows - 1, pre0)

    def residual(s_ref, f_ref, off, d):
        def rest(i):
            row = get(f_ref, off + i)
            n = nb(get(f_ref, off + i - 1), row, get(f_ref, off + i + 1))
            return [s - d * f + v for s, f, v in zip(get(s_ref, off + i), row, n)]

        def coarse(i):
            a, b = rest(2 * i), rest(2 * i + 1)
            c = [x + y for x, y in zip(a, b)]
            return [c[2 * r] + c[2 * r + 1] for r in range(len(c) // 2)]
        return coarse

    coarse0 = residual(s0, f0, H0, d0)
    right1 = lambda i, mask: put(s1, H1 + i, coarse0(i), mask)
    over(1, rows1, rows1 - 1, right1, 2)

    pl.when(has[2])(halo_down.wait_recv)
    pl.when(has[0])(halo_up.wait_recv)
    over(-H0, rows, 0, source)
    over(rows, rows, rows + H0, source)
    over(-5, rows, 1, pre0)
    over(rows - 1, rows, rows + 5, pre0)
    over(-2, rows1, 1, right1)
    over(rows1 - 1, rows1, rows1 + 2, right1)

    one_down = remote(s1.at[pl.ds(H1 + 2, 3)], s1.at[pl.ds(H1 + rows1 + 2, 3)], 2, (group, band - 1))
    one_up = remote(s1.at[pl.ds(H1 + rows1 - 5, 3)], s1.at[pl.ds(0, 3)], 3, (group, band + 1))
    pl.when(has[0])(one_down.start)
    pl.when(has[2])(one_up.start)

    d1, w1 = diag(1)
    pre1 = pre(s1, f1, H1, w1)
    over(-1, rows1, rows1 + 1, pre1, 8)
    coarse1 = residual(s1, f1, H1, d1)
    over(0, rows2, rows2, lambda i, mask: put(s2, HC + i, coarse1(i), mask), 4)

    own2 = s2.at[pl.ds(HC, rows2)]
    gather = []
    for n, (ok, off) in enumerate(zip(has, offsets)):
        c = remote(own2, s2.at[pl.ds(HC - off * rows2, rows2)], 4 + n, (group, band + off))
        pl.when(ok)(c.start)
        gather.append(c)

    pl.when(has[2])(one_down.wait_recv)
    pl.when(has[0])(one_up.wait_recv)

    def outer(a, b, mask):
        def step(i, carry):
            pre1(i, mask)
            return carry
        lax.fori_loop(a, b, step, 0, unroll=True)
    outer(-4, -1, top)
    outer(rows1 + 1, rows1 + 4, bot)

    for n, src in enumerate((2, 3, 0, 1)):
        pl.when(has[src])(gather[n].wait_recv)

    d2, w2 = diag(2)
    far_top = jnp.where(band <= 1, 0.0, 1.0).astype(jnp.float32)
    far_bot = jnp.where(band >= bands - 2, 0.0, 1.0).astype(jnp.float32)

    def mask2(i):
        if i < 0:
            return top if i >= -rows2 else far_top
        if i >= rows2:
            return bot if i < 2 * rows2 else far_bot
        return None

    body = pre(s2, c2a, HC, w2)
    for i in range(-6, rows2 + 6):
        body(i, mask2(i))

    def sweep(s_ref, f_ref, o_ref, off, w):
        def body(i, mask):
            row = get(f_ref, off + i)
            n = nb(get(f_ref, off + i - 1), row, get(f_ref, off + i + 1))
            put(o_ref, off + i, [0.2 * f + w * (s + v) for s, f, v in zip(get(s_ref, off + i), row, n)], mask)
        return body

    a, b = c2a, c2b
    for reach in (5, 4, 3, 2):
        body = sweep(s2, a, b, HC, w2)
        for i in range(-reach, rows2 + reach):
            body(i, mask2(i))
        a, b = b, a
    e2 = a

    def add1(i, mask):
        for t in range(2):
            e = e2[HC + i, 0]
            put(g1, H1 + 2 * i + t, [v + e for v in get(f1, H1 + 2 * i + t)], None)
    over(-2, rows2, rows2 + 2, add1)
    over(-3, rows1, rows1 + 3, sweep(s1, g1, h1, H1, w1), 8)
    over(-2, rows1, rows1 + 2, sweep(s1, h1, g1, H1, w1), 8)

    def add0(i, mask):
        e = get(g1, H1 + i)
        for t in range(2):
            v = get(f0, H0 + 2 * i + t)
            put(g0, H0 + 2 * i + t, [v[r] + e[r // 2] for r in range(4)], None)
    over(-2, rows1, rows1 + 2, add0)
    first0 = sweep(s0, g0, h0, H0, w0)
    last0 = sweep(s0, h0, g0, H0, w0)

    def to_stream(i, mask):
        put(st0, H0 + i, [swap(v) + sgn * v for v in get(g0, H0 + i)], None)

    drag = jnp.where(sub, DRAG, 0.0).astype(jnp.float32)

    part = 8

    def advance(base, i, mask):
        st, su, sd = get(st0, H0 + i), get(st0, H0 + i - 1), get(st0, H0 + i + 1)
        qq, qu, qd = get(q, H0 + i), get(q, H0 + i - 1), get(q, H0 + i + 1)
        sl, sr = sides(st)
        ql, qr = sides(qq)
        for r in range(4):
            sx = 0.5 * (sr[r] - sl[r])
            sy = 0.5 * (sd[r] - su[r])
            qx = 0.5 * (qr[r] - ql[r])
            qy = 0.5 * (qd[r] - qu[r])
            lap = WY * (su[r] + sd[r]) + WX * (sl[r] + sr[r]) - 4.0 * st[r]
            v = qq[r] - STEP * (sx * qy - sy * qx + BETA * sx + drag * lap)
            for kb in range(blocks):
                tr[r, kb, pl.ds(base + i, 8, stride=part), :] = v[:, kb * quarter:(kb + 1) * quarter]
    made = [-2, -1, 0]
    shares, stores = [], []
    for c in range(rows // part):
        end = (c + 1) * part
        over(made[0], rows, end + 2, first0)
        over(made[1], rows, end + 1, last0)
        over(made[1], rows, end + 1, to_stream)
        base = c * part * 7
        over(made[2], rows, end, functools.partial(advance, base), 2)
        made = [end + 2, end + 1, end]
        m = pl.ds(c * part * 8, part * 8)
        here = pl.ds(c * part, part)
        for kb in range(blocks):
            a = jnp.concatenate([tr[r, kb, m] for r in range(4)], axis=1)
            hi = a.astype(jnp.bfloat16)
            lo = (a - hi.astype(jnp.float32)).astype(jnp.bfloat16)
            o = jnp.dot(hi, inv[...], preferred_element_type=jnp.float32)
            o = o + jnp.dot(lo, inv[...], preferred_element_type=jnp.float32)
            for l in range(2):
                for s in range(slots):
                    n = (l * slots + s) * part
                    ov[s, l, here, kb * size:(kb + 1) * size] = o[n:n + part]
        share = remote(ov.at[slots - 1, :, here], out_hbm.at[0, :, here], 8 + c, (group + 1, band))
        pl.when(above)(share.start)
        shares.append((above, share))
        own = pl.ds(1, slots - 1)
        keep = pltpu.make_async_copy(ov.at[own, :, here], out_hbm.at[own, :, here], out_sem.at[2 * c])
        keep.start()
        lone = pltpu.make_async_copy(ov.at[0, :, here], out_hbm.at[0, :, here], out_sem.at[2 * c + 1])
        pl.when(group == 0)(lone.start)
        stores.append((keep, lone))

    for keep, lone in stores:
        keep.wait()
        pl.when(group == 0)(lone.wait)
    for ok, c in ((has[0], halo_down), (has[2], halo_up), (has[0], one_down), (has[2], one_up),
                  *shares, *zip(has, gather)):
        pl.when(ok)(c.wait_send)
    for _, c in shares:
        pl.when(below)(c.wait_recv)


def per_device(states, counts):
    slots, layers, rows, nx = states.shape
    bands, groups = lax.axis_size("band"), lax.axis_size("particle")
    rows1, rows2, lanes = rows // 2, rows // 4, nx // 4
    f32 = jnp.float32
    level0 = pltpu.VMEM((rows + 2 * H0, 4, 8, lanes), f32)
    level1 = pltpu.VMEM((rows1 + 2 * H1, 2, 8, lanes), f32)
    level2 = pltpu.VMEM((rows2 + 2 * HC, 1, 8, lanes), f32)
    return pl.pallas_call(
        functools.partial(kernel, bands, groups, slots, rows),
        out_shape=jax.ShapeDtypeStruct(states.shape, states.dtype),
        in_specs=[pl.BlockSpec(memory_space=pltpu.SMEM), pl.BlockSpec(memory_space=pl.ANY)],
        out_specs=pl.BlockSpec(memory_space=pl.ANY),
        scratch_shapes=[
            pltpu.VMEM(states.shape, f32),
            pltpu.VMEM(states.shape, f32),
            pltpu.VMEM((512, 512), jnp.bfloat16),
            pltpu.VMEM((512, 512), jnp.bfloat16),
            pltpu.VMEM((4, nx // 512, 8 * rows, 128), f32),
            level0, level0, level0, level0, level0, level0,
            level1, level1, level1, level1,
            level2, level2, level2,
            pltpu.SemaphoreType.DMA((slots,)),
            pltpu.SemaphoreType.DMA((rows // 4,)),
            pltpu.SemaphoreType.DMA((8 + rows // 8,)),
            pltpu.SemaphoreType.DMA((8 + rows // 8,)),
        ],
        compiler_params=pltpu.CompilerParams(
            collective_id=0, has_side_effects=True, vmem_limit_bytes=64 * 1024 * 1024 - 256 * 1024
        ),
    )(counts, states)


def solution(mesh):
    in_specs = (P("particle", None, "band", None), P())
    out_specs = P("particle", None, "band", None)
    return jax.shard_map(
        per_device, mesh=mesh, in_specs=in_specs, out_specs=out_specs, check_vma=False
    )
```

```python
import functools

import jax
import jax.numpy as jnp
from jax import lax
from jax.experimental import pallas as pl
from jax.experimental.pallas import tpu as pltpu
from jax.sharding import PartitionSpec as P

MESH = pl.DeviceIdType.MESH
DEFORM = 0.1
RELAX = 0.8
BETA = 0.5
DRAG = 0.2
STEP = 0.5
WY = 1.8
WX = 0.2
H0 = 6
H1 = 5
HC = 8


def lane_roll(a, steps):
    return pltpu.roll(a, steps % a.shape[-1], axis=a.ndim - 1)


def sides(row):
    n = len(row)
    left = [row[r - 1] if r else lane_roll(row[n - 1], 1) for r in range(n)]
    right = [row[r + 1] if r < n - 1 else lane_roll(row[0], -1) for r in range(n)]
    return left, right


def nb(above, row, below):
    left, right = sides(row)
    return [
        WY * (above[r] + below[r]) + WX * (left[r] + right[r]) for r in range(len(row))
    ]


def kernel(bands, groups, slots, rows, counts, x_hbm, out_hbm,
           xv, ov, fwd, inv, tr, q, s0, f0, g0, h0, st0, s1, f1, g1, h1, s2, c2a, c2b,
           in_sem, out_sem, send_sem, recv_sem):
    band = lax.axis_index("band")
    group = lax.axis_index("particle")
    rows1, rows2 = rows // 2, rows // 4
    has = [band >= 1, band >= 2, band < bands - 1, band < bands - 2]
    offsets = [-1, -2, 1, 2]
    below, above = group >= 1, group < groups - 1

    barrier = pltpu.get_barrier_semaphore()
    expected = jnp.int32(0)
    for ok, off in zip(has, offsets):
        expected += jnp.where(ok, 1, 0)

        @pl.when(ok)
        def _():
            pl.semaphore_signal(barrier, inc=1, device_id=(group, band + off), device_id_type=MESH)
    for ok, off in ((below, -1), (above, 1)):
        expected += jnp.where(ok, 1, 0)

        @pl.when(ok)
        def _():
            pl.semaphore_signal(barrier, inc=1, device_id=(group + off, band), device_id_type=MESH)

    loads = [pltpu.make_async_copy(x_hbm.at[j], xv.at[j], in_sem.at[j]) for j in range(slots)]
    for c in loads:
        c.start()

    size = fwd.shape[0]
    quarter = size // 4
    i0 = lax.broadcasted_iota(jnp.int32, (size, size), 0)
    i1 = lax.broadcasted_iota(jnp.int32, (size, size), 1)
    fwd[...] = jnp.where(i0 == 4 * (i1 % quarter) + i1 // quarter, 1.0, 0.0).astype(jnp.bfloat16)
    inv[...] = jnp.where(i1 == 4 * (i0 % quarter) + i0 // quarter, 1.0, 0.0).astype(jnp.bfloat16)

    first = group * slots
    total = jnp.int32(0)
    ancestor = [jnp.int32(0)] * slots
    for i in range(counts.shape[0]):
        total = total + counts[i]
        for j in range(slots):
            ancestor[j] = ancestor[j] + jnp.where(total <= first + j, 1, 0)
    local = [jnp.clip(a - first, 0, slots - 1) for a in ancestor]

    zero = lambda ref, lo, n: ref.__setitem__(pl.ds(lo, n), jnp.zeros((n,) + ref.shape[1:], jnp.float32))

    @pl.when(band == 0)
    def _():
        zero(q, 0, H0)
        zero(s1, 0, 3)
        zero(s2, HC - rows2, rows2)

    @pl.when(band <= 1)
    def _():
        zero(s2, HC - 2 * rows2, rows2)

    @pl.when(band == bands - 1)
    def _():
        zero(q, H0 + rows, H0)
        zero(s1, H1 + rows1 + 2, 3)
        zero(s2, HC + rows2, rows2)

    @pl.when(band >= bands - 2)
    def _():
        zero(s2, HC + 2 * rows2, rows2)

    for c in loads:
        c.wait()

    blocks = xv.shape[-1] // size
    for kb in range(blocks):
        cols = pl.ds(kb * size, size)
        a = jnp.concatenate([xv[local[s], l, :, cols] for l in range(2) for s in range(slots)], axis=0)
        hi = a.astype(jnp.bfloat16)
        lo = (a - hi.astype(jnp.float32)).astype(jnp.bfloat16)
        o = jnp.dot(hi, fwd[...], preferred_element_type=jnp.float32)
        o = o + jnp.dot(lo, fwd[...], preferred_element_type=jnp.float32)
        for r in range(4):
            tr[r, kb] = o[:, r * quarter:(r + 1) * quarter]

    lanes = blocks * quarter
    for y in range(rows):
        for r in range(4):
            for kb in range(blocks):
                q[H0 + y, r, :, kb * quarter:(kb + 1) * quarter] = tr[r, kb, pl.ds(y, 8, stride=rows), :]

    pl.semaphore_wait(barrier, expected)

    def remote(src, dst, sem, dev):
        return pltpu.make_async_remote_copy(
            src_ref=src, dst_ref=dst, send_sem=send_sem.at[sem], recv_sem=recv_sem.at[sem],
            device_id=dev, device_id_type=MESH)

    half = H0 // 2
    spare = 8 + rows // 8
    halos_down, halos_up = [], []
    for k in range(2):
        lo = H0 + k * half
        hi = H0 + rows - (k + 1) * half
        d = remote(q.at[pl.ds(lo, half)], q.at[pl.ds(lo + rows, half)], (0, spare)[k], (group, band - 1))
        u = remote(q.at[pl.ds(hi, half)], q.at[pl.ds(hi - rows, half)], (1, spare + 1)[k], (group, band + 1))
        pl.when(has[0])(d.start)
        pl.when(has[2])(u.start)
        halos_down.append(d)
        halos_up.append(u)

    sub = lax.broadcasted_iota(jnp.int32, (8, lanes), 0) >= slots
    sgn = jnp.where(sub, -1.0, 1.0).astype(jnp.float32)

    def diag(level):
        d = jnp.where(sub, 4.0 + DEFORM * 4.0 ** level, 4.0).astype(jnp.float32)
        return d, RELAX / d

    def swap(v):
        return pltpu.roll(v, slots, axis=0)

    def get(ref, i):
        return [ref[i, r] for r in range(ref.shape[1])]

    def put(ref, i, vals, mask):
        for r, v in enumerate(vals):
            ref[i, r] = v if mask is None else v * mask

    top = jnp.where(band == 0, 0.0, 1.0).astype(jnp.float32)
    bot = jnp.where(band == bands - 1, 0.0, 1.0).astype(jnp.float32)

    def over(lo, n, hi, body, unroll=4):
        parts = ((lo, min(hi, 0), top, True), (max(lo, 0), min(hi, n), None, unroll),
                 (max(lo, n), hi, bot, True))
        for a, b, mask, u in parts:
            if b > a:
                def step(i, carry, mask=mask):
                    body(i, mask)
                    return carry
                if u is not True:
                    u = max(k for k in range(1, u + 1) if (b - a) % k == 0)
                lax.fori_loop(a, b, step, 0, unroll=u)

    d0, w0 = diag(0)

    def source(i, mask):
        row = get(q, H0 + i)
        put(s0, H0 + i, [-0.5 * (swap(v) + sgn * v) for v in row], None)
    over(0, rows, rows, source)

    def pre(s_ref, f_ref, off, w):
        wa, wb = 1.2 * w, w * w

        def body(i, mask):
            row = get(s_ref, off + i)
            n = nb(get(s_ref, off + i - 1), row, get(s_ref, off + i + 1))
            put(f_ref, off + i, [wa * s + wb * v for s, v in zip(row, n)], mask)
        return body

    pre0 = pre(s0, f0, H0, w0)
    over(1, rows, rows - 1, pre0)

    def residual(s_ref, f_ref, off, d):
        def rest(i):
            row = get(f_ref, off + i)
            n = nb(get(f_ref, off + i - 1), row, get(f_ref, off + i + 1))
            return [s - d * f + v for s, f, v in zip(get(s_ref, off + i), row, n)]

        def coarse(i):
            a, b = rest(2 * i), rest(2 * i + 1)
            c = [x + y for x, y in zip(a, b)]
            return [c[2 * r] + c[2 * r + 1] for r in range(len(c) // 2)]
        return coarse

    coarse0 = residual(s0, f0, H0, d0)
    right1 = lambda i, mask: put(s1, H1 + i, coarse0(i), mask)
    over(1, rows1, rows1 - 1, right1, 2)

    for d, u in zip(halos_down, halos_up):
        pl.when(has[2])(d.wait_recv)
        pl.when(has[0])(u.wait_recv)
    over(-H0, rows, 0, source)
    over(rows, rows, rows + H0, source)
    over(-5, rows, 1, pre0)
    over(rows - 1, rows, rows + 5, pre0)
    over(-2, rows1, 1, right1)
    over(rows1 - 1, rows1, rows1 + 2, right1)

    one_down = remote(s1.at[pl.ds(H1 + 2, 3)], s1.at[pl.ds(H1 + rows1 + 2, 3)], 2, (group, band - 1))
    one_up = remote(s1.at[pl.ds(H1 + rows1 - 5, 3)], s1.at[pl.ds(0, 3)], 3, (group, band + 1))
    pl.when(has[0])(one_down.start)
    pl.when(has[2])(one_up.start)

    d1, w1 = diag(1)
    pre1 = pre(s1, f1, H1, w1)
    over(-1, rows1, rows1 + 1, pre1, 8)
    coarse1 = residual(s1, f1, H1, d1)
    over(0, rows2, rows2, lambda i, mask: put(s2, HC + i, coarse1(i), mask), 4)

    gather = []
    for n, (ok, off) in enumerate(zip(has, offsets)):
        skip = 1 if abs(off) == 2 else 0
        src = skip if off > 0 else 0
        c = remote(s2.at[pl.ds(HC + src, rows2 - skip)],
                   s2.at[pl.ds(HC - off * rows2 + src, rows2 - skip)], 4 + n, (group, band + off))
        pl.when(ok)(c.start)
        gather.append(c)

    pl.when(has[2])(one_down.wait_recv)
    pl.when(has[0])(one_up.wait_recv)

    def outer(a, b, mask):
        def step(i, carry):
            pre1(i, mask)
            return carry
        lax.fori_loop(a, b, step, 0, unroll=True)
    outer(-4, -1, top)
    outer(rows1 + 1, rows1 + 4, bot)

    for n, src in enumerate((2, 3, 0, 1)):
        pl.when(has[src])(gather[n].wait_recv)

    d2, w2 = diag(2)
    far_top = jnp.where(band <= 1, 0.0, 1.0).astype(jnp.float32)
    far_bot = jnp.where(band >= bands - 2, 0.0, 1.0).astype(jnp.float32)

    def mask2(i):
        if i < 0:
            return top if i >= -rows2 else far_top
        if i >= rows2:
            return bot if i < 2 * rows2 else far_bot
        return None

    body = pre(s2, c2a, HC, w2)
    for i in range(-6, rows2 + 6):
        body(i, mask2(i))

    def sweep(s_ref, f_ref, o_ref, off, w):
        def body(i, mask):
            row = get(f_ref, off + i)
            n = nb(get(f_ref, off + i - 1), row, get(f_ref, off + i + 1))
            put(o_ref, off + i, [0.2 * f + w * (s + v) for s, f, v in zip(get(s_ref, off + i), row, n)], mask)
        return body

    a, b = c2a, c2b
    for reach in (5, 4, 3, 2):
        body = sweep(s2, a, b, HC, w2)
        for i in range(-reach, rows2 + reach):
            body(i, mask2(i))
        a, b = b, a
    e2 = a

    def add1(i, mask):
        for t in range(2):
            e = e2[HC + i, 0]
            put(g1, H1 + 2 * i + t, [v + e for v in get(f1, H1 + 2 * i + t)], None)
    over(-2, rows2, rows2 + 2, add1)
    over(-3, rows1, rows1 + 3, sweep(s1, g1, h1, H1, w1), 8)
    over(-2, rows1, rows1 + 2, sweep(s1, h1, g1, H1, w1), 8)

    def add0(i, mask):
        e = get(g1, H1 + i)
        for t in range(2):
            v = get(f0, H0 + 2 * i + t)
            put(g0, H0 + 2 * i + t, [v[r] + e[r // 2] for r in range(4)], None)
    over(-2, rows1, rows1 + 2, add0)
    first0 = sweep(s0, g0, h0, H0, w0)
    last0 = sweep(s0, h0, g0, H0, w0)

    def to_stream(i, mask):
        put(st0, H0 + i, [swap(v) + sgn * v for v in get(g0, H0 + i)], None)

    drag = jnp.where(sub, DRAG, 0.0).astype(jnp.float32)

    part = 8

    def advance(base, i, mask):
        st, su, sd = get(st0, H0 + i), get(st0, H0 + i - 1), get(st0, H0 + i + 1)
        qq, qu, qd = get(q, H0 + i), get(q, H0 + i - 1), get(q, H0 + i + 1)
        sl, sr = sides(st)
        ql, qr = sides(qq)
        for r in range(4):
            sx = 0.5 * (sr[r] - sl[r])
            sy = 0.5 * (sd[r] - su[r])
            qx = 0.5 * (qr[r] - ql[r])
            qy = 0.5 * (qd[r] - qu[r])
            lap = WY * (su[r] + sd[r]) + WX * (sl[r] + sr[r]) - 4.0 * st[r]
            v = qq[r] - STEP * (sx * qy - sy * qx + BETA * sx + drag * lap)
            for kb in range(blocks):
                tr[r, kb, pl.ds(base + i, 8, stride=part), :] = v[:, kb * quarter:(kb + 1) * quarter]
    made = [-2, -1, 0]
    shares, stores = [], []
    for c in range(rows // part):
        end = (c + 1) * part
        over(made[0], rows, end + 2, first0)
        over(made[1], rows, end + 1, last0)
        over(made[1], rows, end + 1, to_stream)
        base = c * part * 7
        over(made[2], rows, end, functools.partial(advance, base), 2)
        made = [end + 2, end + 1, end]
        m = pl.ds(c * part * 8, part * 8)
        here = pl.ds(c * part, part)
        for kb in range(blocks):
            a = jnp.concatenate([tr[r, kb, m] for r in range(4)], axis=1)
            hi = a.astype(jnp.bfloat16)
            lo = (a - hi.astype(jnp.float32)).astype(jnp.bfloat16)
            o = jnp.dot(hi, inv[...], preferred_element_type=jnp.float32)
            o = o + jnp.dot(lo, inv[...], preferred_element_type=jnp.float32)
            for l in range(2):
                for s in range(slots):
                    n = (l * slots + s) * part
                    ov[s, l, here, kb * size:(kb + 1) * size] = o[n:n + part]
        share = remote(ov.at[slots - 1, :, here], out_hbm.at[0, :, here], 8 + c, (group + 1, band))
        pl.when(above)(share.start)
        shares.append((above, share))
        own = pl.ds(1, slots - 1)
        keep = pltpu.make_async_copy(ov.at[own, :, here], out_hbm.at[own, :, here], out_sem.at[2 * c])
        keep.start()
        lone = pltpu.make_async_copy(ov.at[0, :, here], out_hbm.at[0, :, here], out_sem.at[2 * c + 1])
        pl.when(group == 0)(lone.start)
        stores.append((keep, lone))

    for keep, lone in stores:
        keep.wait()
        pl.when(group == 0)(lone.wait)
    for ok, c in (*((has[0], d) for d in halos_down), *((has[2], u) for u in halos_up), (has[0], one_down), (has[2], one_up),
                  *shares, *zip(has, gather)):
        pl.when(ok)(c.wait_send)
    for _, c in shares:
        pl.when(below)(c.wait_recv)


def per_device(states, counts):
    slots, layers, rows, nx = states.shape
    bands, groups = lax.axis_size("band"), lax.axis_size("particle")
    rows1, rows2, lanes = rows // 2, rows // 4, nx // 4
    f32 = jnp.float32
    level0 = pltpu.VMEM((rows + 2 * H0, 4, 8, lanes), f32)
    level1 = pltpu.VMEM((rows1 + 2 * H1, 2, 8, lanes), f32)
    level2 = pltpu.VMEM((rows2 + 2 * HC, 1, 8, lanes), f32)
    return pl.pallas_call(
        functools.partial(kernel, bands, groups, slots, rows),
        out_shape=jax.ShapeDtypeStruct(states.shape, states.dtype),
        in_specs=[pl.BlockSpec(memory_space=pltpu.SMEM), pl.BlockSpec(memory_space=pl.ANY)],
        out_specs=pl.BlockSpec(memory_space=pl.ANY),
        scratch_shapes=[
            pltpu.VMEM(states.shape, f32),
            pltpu.VMEM(states.shape, f32),
            pltpu.VMEM((512, 512), jnp.bfloat16),
            pltpu.VMEM((512, 512), jnp.bfloat16),
            pltpu.VMEM((4, nx // 512, 8 * rows, 128), f32),
            level0, level0, level0, level0, level0, level0,
            level1, level1, level1, level1,
            level2, level2, level2,
            pltpu.SemaphoreType.DMA((slots,)),
            pltpu.SemaphoreType.DMA((rows // 4,)),
            pltpu.SemaphoreType.DMA((10 + rows // 8,)),
            pltpu.SemaphoreType.DMA((10 + rows // 8,)),
        ],
        compiler_params=pltpu.CompilerParams(
            collective_id=0, has_side_effects=True, vmem_limit_bytes=64 * 1024 * 1024 - 256 * 1024
        ),
    )(counts, states)


def solution(mesh):
    in_specs = (P("particle", None, "band", None), P())
    out_specs = P("particle", None, "band", None)
    return jax.shard_map(
        per_device, mesh=mesh, in_specs=in_specs, out_specs=out_specs, check_vma=False
    )
```

```python
import functools

import jax
import jax.numpy as jnp
from jax import lax
from jax.experimental import pallas as pl
from jax.experimental.pallas import tpu as pltpu
from jax.sharding import PartitionSpec as P

MESH = pl.DeviceIdType.MESH
DEFORM = 0.1
RELAX = 0.8
BETA = 0.5
DRAG = 0.2
STEP = 0.5
WY = 1.8
WX = 0.2
H0 = 6
H1 = 5
HC = 8


def lane_roll(a, steps):
    return pltpu.roll(a, steps % a.shape[-1], axis=a.ndim - 1)


def sides(row):
    n = len(row)
    left = [row[r - 1] if r else lane_roll(row[n - 1], 1) for r in range(n)]
    right = [row[r + 1] if r < n - 1 else lane_roll(row[0], -1) for r in range(n)]
    return left, right


def nb(above, row, below):
    left, right = sides(row)
    return [
        WY * (above[r] + below[r]) + WX * (left[r] + right[r]) for r in range(len(row))
    ]


def kernel(bands, groups, slots, rows, counts, x_hbm, out_hbm,
           xv, ov, fwd, inv, tr, q, s0, f0, g0, h0, st0, s1, f1, g1, h1, s2, c2a, c2b,
           in_sem, out_sem, send_sem, recv_sem):
    band = lax.axis_index("band")
    group = lax.axis_index("particle")
    rows1, rows2 = rows // 2, rows // 4
    has = [band >= 1, band >= 2, band < bands - 1, band < bands - 2]
    offsets = [-1, -2, 1, 2]
    below, above = group >= 1, group < groups - 1

    barrier = pltpu.get_barrier_semaphore()
    expected = jnp.int32(0)
    for ok, off in zip(has, offsets):
        expected += jnp.where(ok, 1, 0)

        @pl.when(ok)
        def _():
            pl.semaphore_signal(barrier, inc=1, device_id=(group, band + off), device_id_type=MESH)
    for ok, off in ((below, -1), (above, 1)):
        expected += jnp.where(ok, 1, 0)

        @pl.when(ok)
        def _():
            pl.semaphore_signal(barrier, inc=1, device_id=(group + off, band), device_id_type=MESH)

    loads = [pltpu.make_async_copy(x_hbm.at[j], xv.at[j], in_sem.at[j]) for j in range(slots)]
    for c in loads:
        c.start()

    size = fwd.shape[0]
    quarter = size // 4
    i0 = lax.broadcasted_iota(jnp.int32, (size, size), 0)
    i1 = lax.broadcasted_iota(jnp.int32, (size, size), 1)
    fwd[...] = jnp.where(i0 == 4 * (i1 % quarter) + i1 // quarter, 1.0, 0.0).astype(jnp.bfloat16)
    inv[...] = jnp.where(i1 == 4 * (i0 % quarter) + i0 // quarter, 1.0, 0.0).astype(jnp.bfloat16)

    first = group * slots
    total = jnp.int32(0)
    ancestor = [jnp.int32(0)] * slots
    for i in range(counts.shape[0]):
        total = total + counts[i]
        for j in range(slots):
            ancestor[j] = ancestor[j] + jnp.where(total <= first + j, 1, 0)
    local = [jnp.clip(a - first, 0, slots - 1) for a in ancestor]

    zero = lambda ref, lo, n: ref.__setitem__(pl.ds(lo, n), jnp.zeros((n,) + ref.shape[1:], jnp.float32))

    @pl.when(band == 0)
    def _():
        zero(q, 0, H0)
        zero(s1, 0, 3)
        zero(s2, HC - rows2, rows2)

    @pl.when(band <= 1)
    def _():
        zero(s2, HC - 2 * rows2, rows2)

    @pl.when(band == bands - 1)
    def _():
        zero(q, H0 + rows, H0)
        zero(s1, H1 + rows1 + 2, 3)
        zero(s2, HC + rows2, rows2)

    @pl.when(band >= bands - 2)
    def _():
        zero(s2, HC + 2 * rows2, rows2)

    for c in loads:
        c.wait()

    blocks = xv.shape[-1] // size
    for kb in range(blocks):
        cols = pl.ds(kb * size, size)
        a = jnp.concatenate([xv[local[s], l, :, cols] for l in range(2) for s in range(slots)], axis=0)
        hi = a.astype(jnp.bfloat16)
        lo = (a - hi.astype(jnp.float32)).astype(jnp.bfloat16)
        o = jnp.dot(hi, fwd[...], preferred_element_type=jnp.float32)
        o = o + jnp.dot(lo, fwd[...], preferred_element_type=jnp.float32)
        for r in range(4):
            tr[r, kb] = o[:, r * quarter:(r + 1) * quarter]

    lanes = blocks * quarter
    for y in range(rows):
        for r in range(4):
            for kb in range(blocks):
                q[H0 + y, r, :, kb * quarter:(kb + 1) * quarter] = tr[r, kb, pl.ds(y, 8, stride=rows), :]

    pl.semaphore_wait(barrier, expected)

    def remote(src, dst, sem, dev):
        return pltpu.make_async_remote_copy(
            src_ref=src, dst_ref=dst, send_sem=send_sem.at[sem], recv_sem=recv_sem.at[sem],
            device_id=dev, device_id_type=MESH)

    half = H0 // 2
    spare = 8 + rows // 8
    halos_down, halos_up = [], []
    for k in range(2):
        lo = H0 + k * half
        hi = H0 + rows - (k + 1) * half
        d = remote(q.at[pl.ds(lo, half)], q.at[pl.ds(lo + rows, half)], (0, spare)[k], (group, band - 1))
        u = remote(q.at[pl.ds(hi, half)], q.at[pl.ds(hi - rows, half)], (1, spare + 1)[k], (group, band + 1))
        pl.when(has[0])(d.start)
        pl.when(has[2])(u.start)
        halos_down.append(d)
        halos_up.append(u)

    sub = lax.broadcasted_iota(jnp.int32, (8, lanes), 0) >= slots
    sgn = jnp.where(sub, -1.0, 1.0).astype(jnp.float32)

    def diag(level):
        d = jnp.where(sub, 4.0 + DEFORM * 4.0 ** level, 4.0).astype(jnp.float32)
        return d, RELAX / d

    def swap(v):
        return pltpu.roll(v, slots, axis=0)

    def get(ref, i):
        return [ref[i, r] for r in range(ref.shape[1])]

    def put(ref, i, vals, mask):
        for r, v in enumerate(vals):
            ref[i, r] = v if mask is None else v * mask

    top = jnp.where(band == 0, 0.0, 1.0).astype(jnp.float32)
    bot = jnp.where(band == bands - 1, 0.0, 1.0).astype(jnp.float32)

    def over(lo, n, hi, body, unroll=4):
        parts = ((lo, min(hi, 0), top, True), (max(lo, 0), min(hi, n), None, unroll),
                 (max(lo, n), hi, bot, True))
        for a, b, mask, u in parts:
            if b > a:
                def step(i, carry, mask=mask):
                    body(i, mask)
                    return carry
                if u is not True:
                    u = max(k for k in range(1, u + 1) if (b - a) % k == 0)
                lax.fori_loop(a, b, step, 0, unroll=u)

    d0, w0 = diag(0)

    def source(i, mask):
        row = get(q, H0 + i)
        put(s0, H0 + i, [-0.5 * (swap(v) + sgn * v) for v in row], None)
    over(0, rows, rows, source)

    def pre(s_ref, f_ref, off, w):
        wa, wb = 1.2 * w, w * w

        def body(i, mask):
            row = get(s_ref, off + i)
            n = nb(get(s_ref, off + i - 1), row, get(s_ref, off + i + 1))
            put(f_ref, off + i, [wa * s + wb * v for s, v in zip(row, n)], mask)
        return body

    pre0 = pre(s0, f0, H0, w0)
    over(1, rows, rows - 1, pre0)

    def residual(s_ref, f_ref, off, d):
        def rest(i):
            row = get(f_ref, off + i)
            n = nb(get(f_ref, off + i - 1), row, get(f_ref, off + i + 1))
            return [s - d * f + v for s, f, v in zip(get(s_ref, off + i), row, n)]

        def coarse(i):
            a, b = rest(2 * i), rest(2 * i + 1)
            c = [x + y for x, y in zip(a, b)]
            return [c[2 * r] + c[2 * r + 1] for r in range(len(c) // 2)]
        return coarse

    coarse0 = residual(s0, f0, H0, d0)
    right1 = lambda i, mask: put(s1, H1 + i, coarse0(i), mask)
    over(1, rows1, rows1 - 1, right1, 2)

    def landed(k):
        pl.when(has[2])(halos_down[k].wait_recv)
        pl.when(has[0])(halos_up[k].wait_recv)

    landed(0)
    one_down = remote(s1.at[pl.ds(H1 + 2, 3)], s1.at[pl.ds(H1 + rows1 + 2, 3)], 2, (group, band - 1))
    one_up = remote(s1.at[pl.ds(H1 + rows1 - 5, 3)], s1.at[pl.ds(0, 3)], 3, (group, band + 1))
    pl.when(has[0])(one_down.start)
    pl.when(has[2])(one_up.start)

    over(-half, rows, 0, source)
    over(rows, rows, rows + half, source)
    over(1 - half, rows, 1, pre0)
    over(rows - 1, rows, rows + half - 1, pre0)
    over(0, rows1, 1, right1)
    over(rows1 - 1, rows1, rows1, right1)
    landed(1)
    over(-H0, rows, -half, source)
    over(rows + half, rows, rows + H0, source)
    over(-5, rows, 1 - half, pre0)
    over(rows + half - 1, rows, rows + 5, pre0)
    over(-2, rows1, 0, right1)
    over(rows1, rows1, rows1 + 2, right1)

    d1, w1 = diag(1)
    pre1 = pre(s1, f1, H1, w1)
    over(-1, rows1, rows1 + 1, pre1, 8)
    coarse1 = residual(s1, f1, H1, d1)
    over(0, rows2, rows2, lambda i, mask: put(s2, HC + i, coarse1(i), mask), 4)

    gather = []
    for n, (ok, off) in enumerate(zip(has, offsets)):
        skip = 1 if abs(off) == 2 else 0
        src = skip if off > 0 else 0
        c = remote(s2.at[pl.ds(HC + src, rows2 - skip)],
                   s2.at[pl.ds(HC - off * rows2 + src, rows2 - skip)], 4 + n, (group, band + off))
        pl.when(ok)(c.start)
        gather.append(c)

    pl.when(has[2])(one_down.wait_recv)
    pl.when(has[0])(one_up.wait_recv)

    def outer(a, b, mask):
        def step(i, carry):
            pre1(i, mask)
            return carry
        lax.fori_loop(a, b, step, 0, unroll=True)
    outer(-4, -1, top)
    outer(rows1 + 1, rows1 + 4, bot)

    for n, src in enumerate((2, 3, 0, 1)):
        pl.when(has[src])(gather[n].wait_recv)

    d2, w2 = diag(2)
    far_top = jnp.where(band <= 1, 0.0, 1.0).astype(jnp.float32)
    far_bot = jnp.where(band >= bands - 2, 0.0, 1.0).astype(jnp.float32)

    def mask2(i):
        if i < 0:
            return top if i >= -rows2 else far_top
        if i >= rows2:
            return bot if i < 2 * rows2 else far_bot
        return None

    body = pre(s2, c2a, HC, w2)
    for i in range(-6, rows2 + 6):
        body(i, mask2(i))

    def sweep(s_ref, f_ref, o_ref, off, w):
        def body(i, mask):
            row = get(f_ref, off + i)
            n = nb(get(f_ref, off + i - 1), row, get(f_ref, off + i + 1))
            put(o_ref, off + i, [0.2 * f + w * (s + v) for s, f, v in zip(get(s_ref, off + i), row, n)], mask)
        return body

    a, b = c2a, c2b
    for reach in (5, 4, 3, 2):
        body = sweep(s2, a, b, HC, w2)
        for i in range(-reach, rows2 + reach):
            body(i, mask2(i))
        a, b = b, a
    e2 = a

    def add1(i, mask):
        for t in range(2):
            e = e2[HC + i, 0]
            put(g1, H1 + 2 * i + t, [v + e for v in get(f1, H1 + 2 * i + t)], None)
    over(-2, rows2, rows2 + 2, add1)
    over(-3, rows1, rows1 + 3, sweep(s1, g1, h1, H1, w1), 8)
    over(-2, rows1, rows1 + 2, sweep(s1, h1, g1, H1, w1), 8)

    def add0(i, mask):
        e = get(g1, H1 + i)
        for t in range(2):
            v = get(f0, H0 + 2 * i + t)
            put(g0, H0 + 2 * i + t, [v[r] + e[r // 2] for r in range(4)], None)
    over(-2, rows1, rows1 + 2, add0)
    first0 = sweep(s0, g0, h0, H0, w0)
    last0 = sweep(s0, h0, g0, H0, w0)

    def to_stream(i, mask):
        put(st0, H0 + i, [swap(v) + sgn * v for v in get(g0, H0 + i)], None)

    drag = jnp.where(sub, DRAG, 0.0).astype(jnp.float32)

    part = 8

    def advance(base, i, mask):
        st, su, sd = get(st0, H0 + i), get(st0, H0 + i - 1), get(st0, H0 + i + 1)
        qq, qu, qd = get(q, H0 + i), get(q, H0 + i - 1), get(q, H0 + i + 1)
        sl, sr = sides(st)
        ql, qr = sides(qq)
        for r in range(4):
            sx = 0.5 * (sr[r] - sl[r])
            sy = 0.5 * (sd[r] - su[r])
            qx = 0.5 * (qr[r] - ql[r])
            qy = 0.5 * (qd[r] - qu[r])
            lap = WY * (su[r] + sd[r]) + WX * (sl[r] + sr[r]) - 4.0 * st[r]
            v = qq[r] - STEP * (sx * qy - sy * qx + BETA * sx + drag * lap)
            for kb in range(blocks):
                tr[r, kb, pl.ds(base + i, 8, stride=part), :] = v[:, kb * quarter:(kb + 1) * quarter]
    made = [-2, -1, 0]
    shares, stores = [], []
    for c in range(rows // part):
        end = (c + 1) * part
        over(made[0], rows, end + 2, first0)
        over(made[1], rows, end + 1, last0)
        over(made[1], rows, end + 1, to_stream)
        base = c * part * 7
        over(made[2], rows, end, functools.partial(advance, base), 2)
        made = [end + 2, end + 1, end]
        m = pl.ds(c * part * 8, part * 8)
        here = pl.ds(c * part, part)
        for kb in range(blocks):
            a = jnp.concatenate([tr[r, kb, m] for r in range(4)], axis=1)
            hi = a.astype(jnp.bfloat16)
            lo = (a - hi.astype(jnp.float32)).astype(jnp.bfloat16)
            o = jnp.dot(hi, inv[...], preferred_element_type=jnp.float32)
            o = o + jnp.dot(lo, inv[...], preferred_element_type=jnp.float32)
            for l in range(2):
                for s in range(slots):
                    n = (l * slots + s) * part
                    ov[s, l, here, kb * size:(kb + 1) * size] = o[n:n + part]
        share = remote(ov.at[slots - 1, :, here], out_hbm.at[0, :, here], 8 + c, (group + 1, band))
        pl.when(above)(share.start)
        shares.append((above, share))
        own = pl.ds(1, slots - 1)
        keep = pltpu.make_async_copy(ov.at[own, :, here], out_hbm.at[own, :, here], out_sem.at[2 * c])
        keep.start()
        lone = pltpu.make_async_copy(ov.at[0, :, here], out_hbm.at[0, :, here], out_sem.at[2 * c + 1])
        pl.when(group == 0)(lone.start)
        stores.append((keep, lone))

    for keep, lone in stores:
        keep.wait()
        pl.when(group == 0)(lone.wait)
    for ok, c in (*((has[0], d) for d in halos_down), *((has[2], u) for u in halos_up), (has[0], one_down), (has[2], one_up),
                  *shares, *zip(has, gather)):
        pl.when(ok)(c.wait_send)
    for _, c in shares:
        pl.when(below)(c.wait_recv)


def per_device(states, counts):
    slots, layers, rows, nx = states.shape
    bands, groups = lax.axis_size("band"), lax.axis_size("particle")
    rows1, rows2, lanes = rows // 2, rows // 4, nx // 4
    f32 = jnp.float32
    level0 = pltpu.VMEM((rows + 2 * H0, 4, 8, lanes), f32)
    level1 = pltpu.VMEM((rows1 + 2 * H1, 2, 8, lanes), f32)
    level2 = pltpu.VMEM((rows2 + 2 * HC, 1, 8, lanes), f32)
    return pl.pallas_call(
        functools.partial(kernel, bands, groups, slots, rows),
        out_shape=jax.ShapeDtypeStruct(states.shape, states.dtype),
        in_specs=[pl.BlockSpec(memory_space=pltpu.SMEM), pl.BlockSpec(memory_space=pl.ANY)],
        out_specs=pl.BlockSpec(memory_space=pl.ANY),
        scratch_shapes=[
            pltpu.VMEM(states.shape, f32),
            pltpu.VMEM(states.shape, f32),
            pltpu.VMEM((512, 512), jnp.bfloat16),
            pltpu.VMEM((512, 512), jnp.bfloat16),
            pltpu.VMEM((4, nx // 512, 8 * rows, 128), f32),
            level0, level0, level0, level0, level0, level0,
            level1, level1, level1, level1,
            level2, level2, level2,
            pltpu.SemaphoreType.DMA((slots,)),
            pltpu.SemaphoreType.DMA((rows // 4,)),
            pltpu.SemaphoreType.DMA((10 + rows // 8,)),
            pltpu.SemaphoreType.DMA((10 + rows // 8,)),
        ],
        compiler_params=pltpu.CompilerParams(
            collective_id=0, has_side_effects=True, vmem_limit_bytes=64 * 1024 * 1024 - 256 * 1024
        ),
    )(counts, states)


def solution(mesh):
    in_specs = (P("particle", None, "band", None), P())
    out_specs = P("particle", None, "band", None)
    return jax.shard_map(
        per_device, mesh=mesh, in_specs=in_specs, out_specs=out_specs, check_vma=False
    )
```
